32 devices in a mesh: dp: 8 (over z, y), seq: 4 (over x, core).
Axes of the slice: x: 2, y: 2, z: 4, core: 2. Of those that a mesh axis runs over, the one named last changes fastest.
Arguments:
- tokens_in: bfloat16 [16, 2048, 640], P('dp', 'seq'), may hold values from -6 to 6
- segment_ids: int32 [16, 2048], P('dp', 'seq'), may hold values from 0 to 4, as said below
- query_weight: bfloat16 [640, 1024], P('dp', 'seq'), may hold values from -0.25 to 0.25
- key_weight: bfloat16 [640, 256], P('dp', 'seq'), may hold values from -0.25 to 0.25
- value_weight: bfloat16 [640, 256], P('dp', 'seq'), may hold values from -0.25 to 0.25
- out_weight: bfloat16 [1024, 640], P('dp', 'seq'), may hold values from -0.1875 to 0.1875
- gate_weight: bfloat16 [640, 2048], P('dp', 'seq'), may hold values from -0.25 to 0.25
- up_weight: bfloat16 [640, 2048], P('dp', 'seq'), may hold values from -0.25 to 0.25
- down_weight: bfloat16 [2048, 640], P('dp', 'seq'), may hold values from -0.125 to 0.125
- norm_gains: bfloat16 [3072], P(('dp', 'seq')), may hold values from 0.5 to 1.5
- d_output: bfloat16 [16, 2048, 640], P('dp', 'seq'), may hold values from -6 to 6
Outputs:
- output: bfloat16 [16, 2048, 640], P('dp', 'seq')
- grad_input: float32 [16, 2048, 640], P('dp', 'seq')
- grad_query: float32 [640, 1024], P('dp', 'seq')
- grad_key: float32 [640, 256], P('dp', 'seq')
- grad_value: float32 [640, 256], P('dp', 'seq')
- grad_out: float32 [1024, 640], P('dp', 'seq')
- grad_gate: float32 [640, 2048], P('dp', 'seq')
- grad_up: float32 [640, 2048], P('dp', 'seq')
- grad_down: float32 [2048, 640], P('dp', 'seq')
- grad_gains: float32 [3072], P(('dp', 'seq'))
The draws below stay inside these ranges and needn't reach their ends.
Inputs may be any that keep to these rules, and one draw needn't show every extreme that they name: `segment_ids`: along each sequence the ids start at 0 and rise by one at each document boundary. Each block of 512 tokens starting at a multiple of 512 holds at most one boundary, at least 128 tokens from both of its ends.
All inputs are finite; a program needn't handle non-finite values.
Results may differ from the reference program's by a relative error of at most 0.017.
Values may be sent and summed in bfloat16 or wider, within the bound.
A program may use at most 192 MiB of HBM per device.

```python
import math
import jax
import jax.numpy as jnp
from jax import lax

D = 640
NQ = 4
HD = 256
FF = 2048
WINDOW = 512
SEQS = 16
LEN = 2048
GAINS = 3072


def draw_segment_ids(key, part):
    key = jax.random.fold_in(key, 11)
    first_key, second_key, third_key, fourth_key = jax.random.split(key, 4)
    block_count = LEN // WINDOW
    cut_flags = jax.random.randint(first_key, (SEQS, block_count), 0, 2)
    spanning = jax.random.randint(third_key, (), 0, SEQS)
    every_cut = (spanning + 1 + jax.random.randint(fourth_key, (), 0, SEQS - 1)) % SEQS
    seq_number = jnp.arange(SEQS, dtype=jnp.int32)[:, None]
    cut_flags = jnp.where(seq_number == spanning, 0, jnp.where(seq_number == every_cut, 1, cut_flags))
    offsets = jax.random.randint(second_key, (SEQS, block_count), WINDOW // 4, WINDOW - WINDOW // 4 + 1)
    cut_points = jnp.arange(block_count, dtype=jnp.int32)[None, :] * WINDOW + offsets
    token_place = jnp.arange(LEN, dtype=jnp.int32)
    passed = (token_place[None, None, :] >= cut_points[:, :, None]).astype(jnp.int32) * cut_flags[:, :, None]
    return jnp.sum(passed, axis=1).astype(jnp.int32)


def with_spikes(array, own_key, source, target, blocks, factor):
    def block_of(position):
        return (jnp.arange(array.shape[position]) // (array.shape[position] // blocks)).reshape((-1,) + (1,) * (array.ndim - 1 - position))

    near = jax.random.permutation(own_key, blocks)[block_of(target)]
    other_side = (block_of(target) + blocks // 2) % blocks
    return jnp.where((block_of(source) == near) | (block_of(source) == other_side), factor * array, array)


def levels(stream_key, dims, cuts, smallest, high):
    def one(position, parts):
        heights = jax.random.uniform(jax.random.fold_in(jax.random.fold_in(stream_key, 6), position), (parts,), jnp.float32, smallest / len(cuts), high / len(cuts))
        return jnp.repeat(jnp.exp(heights), dims[position] // parts).reshape((-1,) + (1,) * (len(dims) - position - 1))

    level = one(*cuts[0])
    for cut in cuts[1:]:
        level = level * one(*cut)
    return level


def normal_values(own_key, shape, scale, most, shards=(), held_as=jnp.bfloat16):
    gain = levels(own_key, shape, shards, -0.22, 0.18) if shards else 1.0
    values = jax.random.normal(own_key, shape, jnp.float32) * scale * gain
    return jnp.minimum(jnp.maximum(values, -most), most).astype(held_as)


def heavy_noise(rng, shape, deviation, most, pieces, heavy, kind=jnp.bfloat16):
    values = deviation * jax.random.normal(rng, shape, jnp.float32)
    if pieces:
        values = values * levels(rng, shape, pieces, -0.22, 0.18)
    return jnp.clip(with_spikes(values, jax.random.fold_in(rng, 3), *heavy), -most, most).astype(kind)


def setup_inputs(seed: int = 0) -> dict:
    splits = jax.random.split(jax.random.key(seed), 12)
    tokens_in = normal_values(splits[0], (SEQS, LEN, D), 1.0, 6.0, ((0, 8), (1, 4)))
    segment_ids = draw_segment_ids(jax.random.fold_in(splits[11], 71), 0)
    query_weight = normal_values(splits[2], (D, NQ * HD), D ** -0.5, 0.25, ((0, 8), (1, 4)))
    key_weight = normal_values(splits[3], (D, HD), D ** -0.5, 0.25, ((0, 8), (1, 4)))
    value_weight = normal_values(splits[4], (D, HD), D ** -0.5, 0.25, ((0, 8), (1, 4)))
    out_weight = normal_values(splits[5], (NQ * HD, D), (NQ * HD) ** -0.5, 0.1875, ((0, 8), (1, 4)))
    gate_weight = normal_values(splits[6], (D, FF), D ** -0.5, 0.25, ((0, 8), (1, 4)))
    up_weight = normal_values(splits[7], (D, FF), D ** -0.5, 0.25, ((0, 8), (1, 4)))
    down_weight = normal_values(splits[8], (FF, D), FF ** -0.5, 0.125, ((0, 8), (1, 4)))
    norm_gains = jnp.clip(1.0 + 0.1 * jax.random.normal(splits[9], (GAINS,), jnp.float32), 0.5, 1.5).astype(jnp.bfloat16)
    d_output = heavy_noise(splits[10], (SEQS, LEN, D), 1.0, 6.0, ((0, 8), (1, 4)), (1, 2, 4, 2.0))
    return {"tokens_in": tokens_in, "segment_ids": segment_ids, "query_weight": query_weight, "key_weight": key_weight, "value_weight": value_weight, "out_weight": out_weight, "gate_weight": gate_weight, "up_weight": up_weight, "down_weight": down_weight, "norm_gains": norm_gains, "d_output": d_output}


EPSILON = 1e-06
MASKED = -1e+30
HIGH = lax.Precision.HIGHEST

@jax.custom_vjp
def low(v):
    return lax.optimization_barrier(v.astype(jnp.bfloat16)).astype(jnp.float32)

@jax.custom_vjp
def low_back(v):
    return v

def low_keep(v):
    return (low(v), None)

def low_pass(kept, grad):
    return (grad,)

def back_keep(v):
    return (v, None)

def back_low(kept, grad):
    return (low(grad),)
low.defvjp(low_keep, low_pass)
low_back.defvjp(back_keep, back_low)

def rms_scale(values, scales):
    mean_square = lax.optimization_barrier(jnp.mean(values * values, axis=-1, keepdims=True))
    return values * lax.rsqrt(mean_square + EPSILON) * scales

def rotate(values, cosine, sine_table):
    middle = values.shape[-1] // 2
    turned = jnp.concatenate([-values[..., middle:], values[..., :middle]], axis=-1)
    return values * cosine + turned * sine_table

def query_map(raw_part, scales, cosine, sine_table):
    return rotate(rms_scale(raw_part, scales), cosine, sine_table) * (1.0 / math.sqrt(raw_part.shape[-1]))

def key_map(raw_part, scales, cosine, sine_table):
    return rotate(rms_scale(raw_part, scales), cosine, sine_table)

def gated_inner(gate_part, up_part):
    return jax.nn.gelu(gate_part, approximate=True) * up_part

def rotary_tables(positions, head_width):
    frequency = jnp.exp(jnp.arange(head_width // 2, dtype=jnp.float32) * (-2.0 * math.log(10000.0) / head_width))
    angles = positions.astype(jnp.float32)[:, None] * frequency[None, :]
    angles = jnp.concatenate([angles, angles], axis=-1)
    return (jnp.cos(angles), jnp.sin(angles))

def matmul(left_side, right_side):
    return jnp.dot(left_side, right_side, precision=HIGH, preferred_element_type=jnp.float32)

def attention(queries, keys, values, seg_ids):
    block_count = LEN // WINDOW
    padded_keys = jnp.concatenate([jnp.zeros((WINDOW, HD), jnp.float32), keys], axis=0)
    padded_values = jnp.concatenate([jnp.zeros((WINDOW, HD), jnp.float32), values], axis=0)
    padded_ids = jnp.concatenate([jnp.full((WINDOW,), -1, jnp.int32), seg_ids.astype(jnp.int32)])
    row_index = jnp.arange(WINDOW, dtype=jnp.int32)[:, None]
    col_index = jnp.arange(2 * WINDOW, dtype=jnp.int32)[None, :]
    distance = row_index + WINDOW - col_index
    reach = (distance >= 0) & (distance < WINDOW)

    def one_block(block_index):
        block_start = (block_index * WINDOW).astype(jnp.int32)
        query_block = lax.dynamic_slice_in_dim(queries, block_start, WINDOW, 0)
        key_block = lax.dynamic_slice_in_dim(padded_keys, block_start, 2 * WINDOW, 0)
        value_block = lax.dynamic_slice_in_dim(padded_values, block_start, 2 * WINDOW, 0)
        query_ids = lax.dynamic_slice_in_dim(seg_ids.astype(jnp.int32), block_start, WINDOW, 0)
        key_ids = lax.dynamic_slice_in_dim(padded_ids, block_start, 2 * WINDOW, 0)
        scores = low_back(jnp.einsum('qhd,kd->hqk', query_block, key_block, precision=HIGH, preferred_element_type=jnp.float32))
        allowed = reach & (query_ids[:, None] == key_ids[None, :])
        scores = jnp.where(allowed[None], scores, MASKED)
        row_top = lax.optimization_barrier(jnp.max(scores, axis=-1, keepdims=True))
        weights_exp = jnp.exp(scores - row_top)
        prob_weights = low(weights_exp / lax.optimization_barrier(jnp.sum(weights_exp, axis=-1, keepdims=True)))
        return jnp.einsum('hqk,kd->qhd', prob_weights, value_block, precision=HIGH, preferred_element_type=jnp.float32)
    blocks_out = lax.map(jax.checkpoint(one_block), jnp.arange(block_count, dtype=jnp.int32))
    return blocks_out.reshape(LEN, NQ, HD)

def layer(tokens, seg_ids, query_weight, key_weight, value_weight, out_weight, gate_weight, up_weight, down_weight, gains):
    in_scale = gains[0:D]
    attn_scale = gains[D:2 * D]
    pre_scale = gains[2 * D:3 * D]
    post_scale = gains[3 * D:4 * D]
    query_scale = gains[4 * D:4 * D + HD]
    key_scale = gains[4 * D + HD:4 * D + 2 * HD]
    cosine, sine_table = rotary_tables(jnp.arange(LEN, dtype=jnp.int32), HD)
    normed = low(rms_scale(tokens, in_scale))
    query_raw = low_back(matmul(normed, query_weight)).reshape(LEN, NQ, HD)
    key_raw = low_back(matmul(normed, key_weight))
    values = low(low_back(matmul(normed, value_weight)))
    queries = low(query_map(query_raw, query_scale, cosine[:, None, :], sine_table[:, None, :]))
    keys = low(key_map(key_raw, key_scale, cosine, sine_table))
    mixed_heads = low(low_back(attention(queries, keys, values, seg_ids).reshape(LEN, NQ * HD)))
    branch = low_back(matmul(mixed_heads, out_weight))
    residual = tokens + rms_scale(branch, attn_scale)
    inner_normed = low(rms_scale(residual, pre_scale))
    gate_vals = low_back(matmul(inner_normed, gate_weight))
    up_vals = low_back(matmul(inner_normed, up_weight))
    hidden = low(gated_inner(gate_vals, up_vals))
    ffn_vals = low_back(matmul(hidden, down_weight))
    return residual + rms_scale(ffn_vals, post_scale)

def reference(tokens_in, segment_ids, query_weight, key_weight, value_weight, out_weight, gate_weight, up_weight, down_weight, norm_gains, d_output):
    params = (query_weight.astype(jnp.float32), key_weight.astype(jnp.float32), value_weight.astype(jnp.float32), out_weight.astype(jnp.float32), gate_weight.astype(jnp.float32), up_weight.astype(jnp.float32), down_weight.astype(jnp.float32), norm_gains.astype(jnp.float32))
    zero_totals = tuple((jnp.zeros(param.shape, jnp.float32) for param in params))

    def per_sequence(totals, sequence_items):
        tokens, seg_ids, cotangent = sequence_items

        def forward(tokens_float, *weights):
            return layer(tokens_float, seg_ids, *weights)
        result, pullback = jax.vjp(forward, tokens.astype(jnp.float32), *params)
        gradients = pullback(cotangent.astype(jnp.float32))
        updated = tuple((running + gradient for running, gradient in zip(totals, gradients[1:])))
        return (updated, (result.astype(jnp.bfloat16), gradients[0]))
    totals, (outputs, grad_inputs) = lax.scan(per_sequence, zero_totals, (tokens_in, segment_ids, d_output))
    return (outputs, grad_inputs, totals[0], totals[1], totals[2], totals[3], totals[4], totals[5], totals[6], totals[7])
```

```python
from functools import partial
import math

import jax
import jax.numpy as jnp
from jax import lax
from jax.sharding import PartitionSpec as P

D = 640
NQ = 4
HD = 256
FF = 2048
WINDOW = 512
MICRO = 1


EPSILON = 1e-06
MASKED = -1e30


def shifted(block, axis, distance):
    devices = range(lax.axis_size(axis))
    route = [(i - distance, i) for i in devices if i - distance in devices]
    return lax.ppermute(block, axis, route)


def rms_scale(values, scales):
    mean_square = jnp.mean(values * values, axis=-1, keepdims=True)
    return values * lax.rsqrt(mean_square + EPSILON) * scales


def rotate(values, cosine, sine_table):
    middle = values.shape[-1] // 2
    turned = jnp.concatenate([-values[..., middle:], values[..., :middle]], axis=-1)
    return values * cosine + turned * sine_table


def query_map(raw_part, scales, cosine, sine_table):
    return rotate(rms_scale(raw_part, scales), cosine, sine_table) * (
        1.0 / math.sqrt(raw_part.shape[-1])
    )


def key_map(raw_part, scales, cosine, sine_table):
    return rotate(rms_scale(raw_part, scales), cosine, sine_table)


def gated_inner(gate_part, up_part):
    return jax.nn.gelu(gate_part, approximate=True) * up_part


def rotary_tables(positions, head_width):
    frequency = jnp.exp(
        jnp.arange(head_width // 2, dtype=jnp.float32) * (-2.0 * math.log(10000.0) / head_width)
    )
    angles = positions.astype(jnp.float32)[:, None] * frequency[None, :]
    angles = jnp.concatenate([angles, angles], axis=-1)
    return (jnp.cos(angles), jnp.sin(angles))


def rows_product(left_side, right_side):
    return lax.dot_general(
        left_side, right_side, (((0,), (0,)), ((), ())), preferred_element_type=jnp.float32
    )


def times_transposed(left_side, right_side):
    return lax.dot_general(
        left_side, right_side, (((1,), (1,)), ((), ())), preferred_element_type=jnp.float32
    )


def plain_product(left_side, right_side):
    return jnp.dot(left_side, right_side, preferred_element_type=jnp.float32)


def local(
    tokens_in,
    segment_ids,
    query_weight,
    key_weight,
    value_weight,
    out_weight,
    gate_weight,
    up_weight,
    down_weight,
    norm_gains,
    d_output,
):
    seqs_here = tokens_in.shape[0]
    block_len = tokens_in.shape[1]
    per_batch = seqs_here // MICRO
    token_count = per_batch * block_len
    seq_place = lax.axis_index("seq")
    positions = seq_place * block_len + jnp.arange(block_len, dtype=jnp.int32)
    cosine, sine_table = rotary_tables(positions, HD)
    prior_ids = shifted(segment_ids, "seq", 1)
    key_ids = jnp.concatenate([prior_ids, segment_ids], axis=1)
    row_index = jnp.arange(block_len, dtype=jnp.int32)[:, None]
    col_index = jnp.arange(2 * block_len, dtype=jnp.int32)[None, :]
    distance = row_index + block_len - col_index
    reach = (distance >= 0) & (distance < WINDOW) & ((col_index >= block_len) | (seq_place > 0))
    allowed_all = reach[None] & (segment_ids[:, :, None] == key_ids[:, None, :])

    dp_size = lax.axis_size("dp")
    seq_size = lax.axis_size("seq")

    def gathered(block):
        stacked = lax.all_gather(block, "dp", axis=0, tiled=False)
        return lax.all_gather(stacked, "seq", axis=0, tiled=False)

    def columns_joined(stack):
        return stack.transpose(1, 2, 0, 3).reshape(dp_size * stack.shape[2], -1)

    def rows_joined(stack):
        return stack.transpose(0, 2, 1, 3).reshape(seq_size * stack.shape[2], -1)

    def fetch_weights():
        rows_in = query_weight.shape[0]
        query_cols = query_weight.shape[1]
        key_cols = key_weight.shape[1]
        width = query_cols + 2 * key_cols
        gain_rows = -(-norm_gains.shape[0] // width)
        gain_rows = -(-gain_rows // 16) * 16
        gain_block = jnp.pad(norm_gains, (0, gain_rows * width - norm_gains.shape[0])).reshape(
            gain_rows, width
        )
        first = jnp.concatenate(
            [jnp.concatenate([query_weight, key_weight, value_weight], axis=1), gain_block], axis=0
        )
        first = gathered(first)
        second = gathered(out_weight.T)
        third = gathered(jnp.concatenate([gate_weight, up_weight], axis=1))
        fourth = gathered(down_weight.T)
        half = gate_weight.shape[1]
        gains_all = first[:, :, rows_in:].reshape(seq_size, dp_size, -1)[..., : norm_gains.shape[0]]
        return (
            columns_joined(first[:, :, :rows_in, :query_cols]),
            columns_joined(first[:, :, :rows_in, query_cols : query_cols + key_cols]),
            columns_joined(first[:, :, :rows_in, query_cols + key_cols :]),
            rows_joined(second),
            columns_joined(third[..., :half]),
            columns_joined(third[..., half:]),
            rows_joined(fourth),
            gains_all.transpose(1, 0, 2).reshape(-1),
        )

    weights_all = fetch_weights()

    def seq_summed(block):
        return lax.psum_scatter(block, "seq", scatter_dimension=0, tiled=True)

    def dp_summed(block):
        return lax.psum_scatter(block, "dp", scatter_dimension=0, tiled=True)

    def seq_split(block):
        return block.astype(jnp.bfloat16).reshape(seq_size, -1, block.shape[1])

    def dp_split(block):
        return block.reshape(block.shape[0], dp_size, -1).transpose(1, 0, 2)

    out_blocks = []
    grad_blocks = []
    for micro_index in range(MICRO):
        row_lower = micro_index * per_batch
        row_upper = row_lower + per_batch
        weights_now = weights_all
        gains_float = weights_now[7].astype(jnp.float32)
        in_scale = gains_float[0:D]
        attn_scale = gains_float[D : 2 * D]
        pre_scale = gains_float[2 * D : 3 * D]
        post_scale = gains_float[3 * D : 4 * D]
        query_scale = gains_float[4 * D : 4 * D + HD]
        key_scale = gains_float[4 * D + HD : 4 * D + 2 * HD]
        tokens_now = tokens_in[row_lower:row_upper].astype(jnp.float32).reshape(token_count, D)
        normed_vals, input_pull = jax.vjp(rms_scale, tokens_now, in_scale)
        normed = normed_vals.astype(jnp.bfloat16)
        query_raw = plain_product(normed, weights_now[0]).reshape(per_batch, block_len, NQ, HD)
        key_raw = plain_product(normed, weights_now[1]).reshape(per_batch, block_len, HD)
        values_own = (
            plain_product(normed, weights_now[2])
            .astype(jnp.bfloat16)
            .reshape(per_batch, block_len, HD)
        )
        query_vals, query_pull = jax.vjp(
            partial(query_map, cosine=cosine[:, None, :], sine_table=sine_table[:, None, :]),
            query_raw,
            query_scale,
        )
        key_vals, key_pull = jax.vjp(
            partial(key_map, cosine=cosine, sine_table=sine_table), key_raw, key_scale
        )
        queries = query_vals.astype(jnp.bfloat16)
        keys_own = key_vals.astype(jnp.bfloat16)
        prior_pair = shifted(jnp.concatenate([keys_own, values_own], axis=-1), "seq", 1)
        keys_all = jnp.concatenate([prior_pair[..., :HD], keys_own], axis=1)
        values_all = jnp.concatenate([prior_pair[..., HD:], values_own], axis=1)
        allowed = allowed_all[row_lower:row_upper][:, None]
        scores = jnp.einsum("sqhd,skd->shqk", queries, keys_all, preferred_element_type=jnp.float32)
        scores = jnp.where(allowed, scores, MASKED)
        row_top = jnp.max(scores, axis=-1, keepdims=True)
        weights_exp = jnp.exp(scores - row_top)
        row_total = jnp.sum(weights_exp, axis=-1, keepdims=True)
        prob_weights = (weights_exp / row_total).astype(jnp.bfloat16)
        mixed_heads = jnp.einsum(
            "shqk,skd->sqhd", prob_weights, values_all, preferred_element_type=jnp.float32
        )
        mixed_heads = mixed_heads.astype(jnp.bfloat16).reshape(token_count, NQ * HD)
        branch = times_transposed(mixed_heads, weights_now[3])
        post_vals, post_pull = jax.vjp(rms_scale, branch, attn_scale)
        residual = tokens_now + post_vals
        inner_vals, inner_pull = jax.vjp(rms_scale, residual, pre_scale)
        inner_normed = inner_vals.astype(jnp.bfloat16)
        gate_vals = plain_product(inner_normed, weights_now[4])
        up_vals = plain_product(inner_normed, weights_now[5])
        hidden_vals, hidden_pull = jax.vjp(gated_inner, gate_vals, up_vals)
        hidden = hidden_vals.astype(jnp.bfloat16)
        ffn_vals = times_transposed(hidden, weights_now[6])
        final_vals, final_pull = jax.vjp(rms_scale, ffn_vals, post_scale)
        out_blocks.append(
            (residual + final_vals).astype(jnp.bfloat16).reshape(per_batch, block_len, D)
        )
        weights_back = weights_all
        cotangent = d_output[row_lower:row_upper].astype(jnp.float32).reshape(token_count, D)
        d_ffn, d_post_scale = final_pull(cotangent)
        d_ffn = d_ffn.astype(jnp.bfloat16)
        grad_down = seq_summed(rows_product(d_ffn, hidden).astype(jnp.bfloat16))
        d_hidden = plain_product(d_ffn, weights_back[6])
        d_gate, d_up = hidden_pull(d_hidden)
        d_gate = d_gate.astype(jnp.bfloat16)
        d_up = d_up.astype(jnp.bfloat16)
        grad_pair = seq_summed(
            jnp.concatenate(
                [
                    seq_split(rows_product(d_gate, inner_normed)),
                    seq_split(rows_product(d_up, inner_normed)),
                ],
                axis=1,
            )
        )[0]
        d_inner = times_transposed(d_gate, weights_back[4]) + times_transposed(
            d_up, weights_back[5]
        )
        d_resid_part, d_pre_scale = inner_pull(d_inner)
        d_resid = cotangent + d_resid_part
        d_branch, d_attn_scale = post_pull(d_resid)
        d_branch = d_branch.astype(jnp.bfloat16)
        grad_out = seq_summed(rows_product(d_branch, mixed_heads).astype(jnp.bfloat16))
        d_mixed = (
            plain_product(d_branch, weights_back[3])
            .astype(jnp.bfloat16)
            .reshape(per_batch, block_len, NQ, HD)
        )
        scores_again = jnp.einsum(
            "sqhd,skd->shqk", queries, keys_all, preferred_element_type=jnp.float32
        )
        scores_again = jnp.where(allowed, scores_again, MASKED)
        probs_float = jnp.exp(scores_again - row_top) / row_total
        probs_again = probs_float.astype(jnp.bfloat16)
        d_probs = jnp.einsum(
            "sqhd,skd->shqk", d_mixed, values_all, preferred_element_type=jnp.float32
        )
        row_inner = jnp.sum(probs_float * d_probs, axis=-1, keepdims=True)
        d_scores = (probs_float * (d_probs - row_inner)).astype(jnp.bfloat16)
        d_queries = jnp.einsum(
            "shqk,skd->sqhd", d_scores, keys_all, preferred_element_type=jnp.float32
        )
        d_keys = jnp.einsum("shqk,sqhd->skd", d_scores, queries, preferred_element_type=jnp.float32)
        d_values = jnp.einsum(
            "shqk,sqhd->skd", probs_again, d_mixed, preferred_element_type=jnp.float32
        )
        earlier_part = jnp.concatenate([d_keys[:, :block_len], d_values[:, :block_len]], axis=-1).astype(jnp.bfloat16)
        later_pair = shifted(earlier_part, "seq", -1)
        d_keys_own = d_keys[:, block_len:] + later_pair[..., :HD]
        d_values_own = (
            (d_values[:, block_len:] + later_pair[..., HD:])
            .astype(jnp.bfloat16)
            .reshape(token_count, HD)
        )
        d_query_raw, d_query_scale = query_pull(d_queries)
        d_query_raw = d_query_raw.astype(jnp.bfloat16).reshape(token_count, NQ * HD)
        d_key_raw, d_key_scale = key_pull(d_keys_own)
        d_key_raw = d_key_raw.astype(jnp.bfloat16).reshape(token_count, HD)
        grad_query = rows_product(d_query_raw, normed)
        grad_key = rows_product(d_key_raw, normed)
        grad_value = rows_product(d_values_own, normed)
        d_normed = (
            times_transposed(d_query_raw, weights_back[0])
            + times_transposed(d_key_raw, weights_back[1])
            + times_transposed(d_values_own, weights_back[2])
        )
        d_tokens, d_in_scale = input_pull(d_normed)
        grad_blocks.append((d_resid + d_tokens).reshape(per_batch, block_len, D))
        grad_gains = jnp.concatenate(
            [d_in_scale, d_attn_scale, d_pre_scale, d_post_scale, d_query_scale, d_key_scale]
        )
    output = jnp.concatenate(out_blocks, axis=0)
    grad_input = jnp.concatenate(grad_blocks, axis=0)
    gain_count = norm_gains.shape[0]
    gain_rows = -(-(dp_size * gain_count) // (16 * D)) * 16
    gain_part = grad_gains.reshape(dp_size, seq_size, gain_count).transpose(1, 0, 2)
    gain_part = jnp.pad(
        gain_part.reshape(seq_size, -1), ((0, 0), (0, gain_rows * D - dp_size * gain_count))
    ).reshape(seq_size, gain_rows, D)
    last = seq_summed(
        jnp.concatenate(
            [
                seq_split(grad_query),
                seq_split(grad_key),
                seq_split(grad_value),
                gain_part.astype(jnp.bfloat16),
            ],
            axis=1,
        )
    )[0]
    width = last.shape[0] - gain_rows
    gain_now = last[width:].reshape(-1)[: dp_size * gain_count].reshape(dp_size, gain_count)
    extra = -(-gain_count // (16 * width)) * 16
    gain_now = jnp.pad(gain_now, ((0, 0), (0, extra * width - gain_count)))
    last = jnp.concatenate(
        [
            last[:width].T.reshape(dp_size, D // dp_size, width),
            gain_now.reshape(dp_size, extra, width),
        ],
        axis=1,
    )
    last = dp_summed(last)[0].astype(jnp.float32)
    rows_in = query_weight.shape[0]
    query_cols = query_weight.shape[1]
    key_cols = key_weight.shape[1]
    half = gate_weight.shape[1]
    pair_done = dp_summed(grad_pair.T).astype(jnp.float32)
    out_done = dp_summed(dp_split(grad_out))[0].astype(jnp.float32).T
    down_done = dp_summed(dp_split(grad_down))[0].astype(jnp.float32).T
    return (
        output,
        grad_input,
        last[:rows_in, :query_cols],
        last[:rows_in, query_cols : query_cols + key_cols],
        last[:rows_in, query_cols + key_cols :],
        out_done,
        pair_done[:, :half],
        pair_done[:, half:],
        down_done,
        last[rows_in:].reshape(-1)[:gain_count],
    )


def solution(mesh):
    return jax.shard_map(
        local,
        mesh=mesh,
        in_specs=(
            P("dp", "seq", None),
            P("dp", "seq"),
            P("dp", "seq"),
            P("dp", "seq"),
            P("dp", "seq"),
            P("dp", "seq"),
            P("dp", "seq"),
            P("dp", "seq"),
            P("dp", "seq"),
            P(("dp", "seq")),
            P("dp", "seq", None),
        ),
        out_specs=(
            P("dp", "seq", None),
            P("dp", "seq", None),
            P("dp", "seq"),
            P("dp", "seq"),
            P("dp", "seq"),
            P("dp", "seq"),
            P("dp", "seq"),
            P("dp", "seq"),
            P("dp", "seq"),
            P(("dp", "seq")),
        ),
        check_vma=False,
    )
```

```python
from functools import partial
import math

import jax
import jax.numpy as jnp
from jax import lax
from jax.sharding import PartitionSpec as P

D = 640
NQ = 4
HD = 256
FF = 2048
WINDOW = 512
MICRO = 1


EPSILON = 1e-06
MASKED = -1e30


def shifted(block, axis, distance):
    devices = range(lax.axis_size(axis))
    route = [(i - distance, i) for i in devices if i - distance in devices]
    return lax.ppermute(block, axis, route)


def steps_of(axis):
    return lax.axis_size(axis).bit_length() - 1


def swapped(block, axis, step):
    route = [(i, i ^ (1 << step)) for i in range(lax.axis_size(axis))]
    return lax.ppermute(block, axis, route), (lax.axis_index(axis) >> step) & 1


def rms_scale(values, scales):
    mean_square = jnp.mean(values * values, axis=-1, keepdims=True)
    return values * lax.rsqrt(mean_square + EPSILON) * scales


def rotate(values, cosine, sine_table):
    middle = values.shape[-1] // 2
    turned = jnp.concatenate([-values[..., middle:], values[..., :middle]], axis=-1)
    return values * cosine + turned * sine_table


def query_map(raw_part, scales, cosine, sine_table):
    return rotate(rms_scale(raw_part, scales), cosine, sine_table) * (
        1.0 / math.sqrt(raw_part.shape[-1])
    )


def key_map(raw_part, scales, cosine, sine_table):
    return rotate(rms_scale(raw_part, scales), cosine, sine_table)


def gated_inner(gate_part, up_part):
    return jax.nn.gelu(gate_part, approximate=True) * up_part


def rotary_tables(positions, head_width):
    frequency = jnp.exp(
        jnp.arange(head_width // 2, dtype=jnp.float32) * (-2.0 * math.log(10000.0) / head_width)
    )
    angles = positions.astype(jnp.float32)[:, None] * frequency[None, :]
    angles = jnp.concatenate([angles, angles], axis=-1)
    return (jnp.cos(angles), jnp.sin(angles))


def rows_product(left_side, right_side):
    return lax.dot_general(
        left_side, right_side, (((0,), (0,)), ((), ())), preferred_element_type=jnp.float32
    )


def times_transposed(left_side, right_side):
    return lax.dot_general(
        left_side, right_side, (((1,), (1,)), ((), ())), preferred_element_type=jnp.float32
    )


def plain_product(left_side, right_side):
    return jnp.dot(left_side, right_side, preferred_element_type=jnp.float32)


def local(
    tokens_in,
    segment_ids,
    query_weight,
    key_weight,
    value_weight,
    out_weight,
    gate_weight,
    up_weight,
    down_weight,
    norm_gains,
    d_output,
):
    seqs_here = tokens_in.shape[0]
    block_len = tokens_in.shape[1]
    per_batch = seqs_here // MICRO
    token_count = per_batch * block_len
    seq_place = lax.axis_index("seq")
    positions = seq_place * block_len + jnp.arange(block_len, dtype=jnp.int32)
    cosine, sine_table = rotary_tables(positions, HD)
    prior_ids = shifted(segment_ids, "seq", 1)
    key_ids = jnp.concatenate([prior_ids, segment_ids], axis=1)
    row_index = jnp.arange(block_len, dtype=jnp.int32)[:, None]
    col_index = jnp.arange(2 * block_len, dtype=jnp.int32)[None, :]
    distance = row_index + block_len - col_index
    reach = (distance >= 0) & (distance < WINDOW) & ((col_index >= block_len) | (seq_place > 0))
    allowed_all = reach[None] & (segment_ids[:, :, None] == key_ids[:, None, :])

    dp_size = lax.axis_size("dp")
    seq_size = lax.axis_size("seq")

    def gathered(block):
        shape = block.shape
        block = block[None]
        for axis in ("dp", "seq"):
            for step in reversed(range(steps_of(axis))):
                other, mine = swapped(block, axis, step)
                block = jnp.where(
                    mine == 0,
                    jnp.concatenate([block, other], axis=0),
                    jnp.concatenate([other, block], axis=0),
                )
        bits = steps_of("dp") + steps_of("seq")
        block = block.reshape((2,) * bits + shape)
        seq_dims = tuple(reversed(range(steps_of("seq"))))
        dp_dims = tuple(reversed(range(steps_of("seq"), bits)))
        block = block.transpose(seq_dims + dp_dims + (bits, bits + 1))
        return block.reshape((seq_size, dp_size) + shape)

    def columns_joined(stack):
        return stack.transpose(1, 2, 0, 3).reshape(dp_size * stack.shape[2], -1)

    def rows_joined(stack):
        return stack.transpose(0, 2, 1, 3).reshape(seq_size * stack.shape[2], -1)

    def fetch_weights():
        rows_in = query_weight.shape[0]
        query_cols = query_weight.shape[1]
        key_cols = key_weight.shape[1]
        width = query_cols + 2 * key_cols
        gain_rows = -(-norm_gains.shape[0] // width)
        gain_rows = -(-gain_rows // 16) * 16
        gain_block = jnp.pad(norm_gains, (0, gain_rows * width - norm_gains.shape[0])).reshape(
            gain_rows, width
        )
        first = jnp.concatenate(
            [jnp.concatenate([query_weight, key_weight, value_weight], axis=1), gain_block], axis=0
        )
        first = gathered(first)
        second = gathered(out_weight.T)
        third = gathered(jnp.concatenate([gate_weight, up_weight], axis=1))
        fourth = gathered(down_weight.T)
        half = gate_weight.shape[1]
        gains_all = first[:, :, rows_in:].reshape(seq_size, dp_size, -1)[..., : norm_gains.shape[0]]
        return (
            columns_joined(first[:, :, :rows_in, :query_cols]),
            columns_joined(first[:, :, :rows_in, query_cols : query_cols + key_cols]),
            columns_joined(first[:, :, :rows_in, query_cols + key_cols :]),
            rows_joined(second),
            columns_joined(third[..., :half]),
            columns_joined(third[..., half:]),
            rows_joined(fourth),
            gains_all.transpose(1, 0, 2).reshape(-1),
        )

    weights_all = fetch_weights()

    def halved(block, axis):
        rest = block.shape[1:]
        for step in range(steps_of(axis)):
            block = block.reshape((-1, 2) + rest)
            mine = (lax.axis_index(axis) >> step) & 1
            away = jnp.where(mine == 0, block[:, 1], block[:, 0])
            kept = jnp.where(mine == 0, block[:, 0], block[:, 1])
            other, _ = swapped(away, axis, step)
            block = (kept.astype(jnp.float32) + other.astype(jnp.float32)).astype(jnp.bfloat16)
        return block[0]

    def seq_summed(block):
        return halved(block, "seq")

    def dp_summed(block):
        return halved(block, "dp")

    def seq_split(block):
        return block.astype(jnp.bfloat16).reshape(seq_size, -1, block.shape[1])

    def dp_split(block):
        return block.reshape(block.shape[0], dp_size, -1).transpose(1, 0, 2)

    out_blocks = []
    grad_blocks = []
    for micro_index in range(MICRO):
        row_lower = micro_index * per_batch
        row_upper = row_lower + per_batch
        weights_now = weights_all
        gains_float = weights_now[7].astype(jnp.float32)
        in_scale = gains_float[0:D]
        attn_scale = gains_float[D : 2 * D]
        pre_scale = gains_float[2 * D : 3 * D]
        post_scale = gains_float[3 * D : 4 * D]
        query_scale = gains_float[4 * D : 4 * D + HD]
        key_scale = gains_float[4 * D + HD : 4 * D + 2 * HD]
        tokens_now = tokens_in[row_lower:row_upper].astype(jnp.float32).reshape(token_count, D)
        normed_vals, input_pull = jax.vjp(rms_scale, tokens_now, in_scale)
        normed = normed_vals.astype(jnp.bfloat16)
        query_raw = plain_product(normed, weights_now[0]).reshape(per_batch, block_len, NQ, HD)
        key_raw = plain_product(normed, weights_now[1]).reshape(per_batch, block_len, HD)
        values_own = (
            plain_product(normed, weights_now[2])
            .astype(jnp.bfloat16)
            .reshape(per_batch, block_len, HD)
        )
        query_vals, query_pull = jax.vjp(
            partial(query_map, cosine=cosine[:, None, :], sine_table=sine_table[:, None, :]),
            query_raw,
            query_scale,
        )
        key_vals, key_pull = jax.vjp(
            partial(key_map, cosine=cosine, sine_table=sine_table), key_raw, key_scale
        )
        queries = query_vals.astype(jnp.bfloat16)
        keys_own = key_vals.astype(jnp.bfloat16)
        prior_pair = shifted(jnp.concatenate([keys_own, values_own], axis=-1), "seq", 1)
        keys_all = jnp.concatenate([prior_pair[..., :HD], keys_own], axis=1)
        values_all = jnp.concatenate([prior_pair[..., HD:], values_own], axis=1)
        allowed = allowed_all[row_lower:row_upper][:, None]
        scores = jnp.einsum("sqhd,skd->shqk", queries, keys_all, preferred_element_type=jnp.float32)
        scores = jnp.where(allowed, scores, MASKED)
        row_top = jnp.max(scores, axis=-1, keepdims=True)
        weights_exp = jnp.exp(scores - row_top)
        row_total = jnp.sum(weights_exp, axis=-1, keepdims=True)
        prob_weights = (weights_exp / row_total).astype(jnp.bfloat16)
        mixed_heads = jnp.einsum(
            "shqk,skd->sqhd", prob_weights, values_all, preferred_element_type=jnp.float32
        )
        mixed_heads = mixed_heads.astype(jnp.bfloat16).reshape(token_count, NQ * HD)
        branch = times_transposed(mixed_heads, weights_now[3])
        post_vals, post_pull = jax.vjp(rms_scale, branch, attn_scale)
        residual = tokens_now + post_vals
        inner_vals, inner_pull = jax.vjp(rms_scale, residual, pre_scale)
        inner_normed = inner_vals.astype(jnp.bfloat16)
        gate_vals = plain_product(inner_normed, weights_now[4])
        up_vals = plain_product(inner_normed, weights_now[5])
        hidden_vals, hidden_pull = jax.vjp(gated_inner, gate_vals, up_vals)
        hidden = hidden_vals.astype(jnp.bfloat16)
        ffn_vals = times_transposed(hidden, weights_now[6])
        final_vals, final_pull = jax.vjp(rms_scale, ffn_vals, post_scale)
        out_blocks.append(
            (residual + final_vals).astype(jnp.bfloat16).reshape(per_batch, block_len, D)
        )
        weights_back = weights_all
        cotangent = d_output[row_lower:row_upper].astype(jnp.float32).reshape(token_count, D)
        d_ffn, d_post_scale = final_pull(cotangent)
        d_ffn = d_ffn.astype(jnp.bfloat16)
        grad_down = seq_summed(seq_split(rows_product(d_ffn, hidden)))
        d_hidden = plain_product(d_ffn, weights_back[6])
        d_gate, d_up = hidden_pull(d_hidden)
        d_gate = d_gate.astype(jnp.bfloat16)
        d_up = d_up.astype(jnp.bfloat16)
        grad_pair = seq_summed(
            jnp.concatenate(
                [
                    seq_split(rows_product(d_gate, inner_normed)),
                    seq_split(rows_product(d_up, inner_normed)),
                ],
                axis=1,
            )
        )
        d_inner = times_transposed(d_gate, weights_back[4]) + times_transposed(
            d_up, weights_back[5]
        )
        d_resid_part, d_pre_scale = inner_pull(d_inner)
        d_resid = cotangent + d_resid_part
        d_branch, d_attn_scale = post_pull(d_resid)
        d_branch = d_branch.astype(jnp.bfloat16)
        grad_out = seq_summed(seq_split(rows_product(d_branch, mixed_heads)))
        d_mixed = (
            plain_product(d_branch, weights_back[3])
            .astype(jnp.bfloat16)
            .reshape(per_batch, block_len, NQ, HD)
        )
        scores_again = jnp.einsum(
            "sqhd,skd->shqk", queries, keys_all, preferred_element_type=jnp.float32
        )
        scores_again = jnp.where(allowed, scores_again, MASKED)
        probs_float = jnp.exp(scores_again - row_top) / row_total
        probs_again = probs_float.astype(jnp.bfloat16)
        d_probs = jnp.einsum(
            "sqhd,skd->shqk", d_mixed, values_all, preferred_element_type=jnp.float32
        )
        row_inner = jnp.sum(probs_float * d_probs, axis=-1, keepdims=True)
        d_scores = (probs_float * (d_probs - row_inner)).astype(jnp.bfloat16)
        d_queries = jnp.einsum(
            "shqk,skd->sqhd", d_scores, keys_all, preferred_element_type=jnp.float32
        )
        d_keys = jnp.einsum("shqk,sqhd->skd", d_scores, queries, preferred_element_type=jnp.float32)
        d_values = jnp.einsum(
            "shqk,sqhd->skd", probs_again, d_mixed, preferred_element_type=jnp.float32
        )
        earlier_part = jnp.concatenate([d_keys[:, :block_len], d_values[:, :block_len]], axis=-1).astype(jnp.bfloat16)
        later_pair = shifted(earlier_part, "seq", -1)
        d_keys_own = d_keys[:, block_len:] + later_pair[..., :HD]
        d_values_own = (
            (d_values[:, block_len:] + later_pair[..., HD:])
            .astype(jnp.bfloat16)
            .reshape(token_count, HD)
        )
        d_query_raw, d_query_scale = query_pull(d_queries)
        d_query_raw = d_query_raw.astype(jnp.bfloat16).reshape(token_count, NQ * HD)
        d_key_raw, d_key_scale = key_pull(d_keys_own)
        d_key_raw = d_key_raw.astype(jnp.bfloat16).reshape(token_count, HD)
        grad_query = rows_product(d_query_raw, normed)
        grad_key = rows_product(d_key_raw, normed)
        grad_value = rows_product(d_values_own, normed)
        d_normed = (
            times_transposed(d_query_raw, weights_back[0])
            + times_transposed(d_key_raw, weights_back[1])
            + times_transposed(d_values_own, weights_back[2])
        )
        d_tokens, d_in_scale = input_pull(d_normed)
        grad_blocks.append((d_resid + d_tokens).reshape(per_batch, block_len, D))
        grad_gains = jnp.concatenate(
            [d_in_scale, d_attn_scale, d_pre_scale, d_post_scale, d_query_scale, d_key_scale]
        )
    output = jnp.concatenate(out_blocks, axis=0)
    grad_input = jnp.concatenate(grad_blocks, axis=0)
    gain_count = norm_gains.shape[0]
    gain_rows = -(-(dp_size * gain_count) // (16 * D)) * 16
    gain_part = grad_gains.reshape(dp_size, seq_size, gain_count).transpose(1, 0, 2)
    gain_part = jnp.pad(
        gain_part.reshape(seq_size, -1), ((0, 0), (0, gain_rows * D - dp_size * gain_count))
    ).reshape(seq_size, gain_rows, D)
    last = seq_summed(
        jnp.concatenate(
            [
                seq_split(grad_query),
                seq_split(grad_key),
                seq_split(grad_value),
                gain_part.astype(jnp.bfloat16),
            ],
            axis=1,
        )
    )
    width = last.shape[0] - gain_rows
    gain_now = last[width:].reshape(-1)[: dp_size * gain_count].reshape(dp_size, gain_count)
    extra = -(-gain_count // (16 * width)) * 16
    gain_now = jnp.pad(gain_now, ((0, 0), (0, extra * width - gain_count)))
    last = jnp.concatenate(
        [
            last[:width].T.reshape(dp_size, D // dp_size, width),
            gain_now.reshape(dp_size, extra, width),
        ],
        axis=1,
    )
    last = dp_summed(last).astype(jnp.float32)
    rows_in = query_weight.shape[0]
    query_cols = query_weight.shape[1]
    key_cols = key_weight.shape[1]
    half = gate_weight.shape[1]
    pair_done = dp_summed(grad_pair.T.reshape(dp_size, D // dp_size, -1)).astype(jnp.float32)
    out_done = dp_summed(dp_split(grad_out)).astype(jnp.float32).T
    down_done = dp_summed(dp_split(grad_down)).astype(jnp.float32).T
    return (
        output,
        grad_input,
        last[:rows_in, :query_cols],
        last[:rows_in, query_cols : query_cols + key_cols],
        last[:rows_in, query_cols + key_cols :],
        out_done,
        pair_done[:, :half],
        pair_done[:, half:],
        down_done,
        last[rows_in:].reshape(-1)[:gain_count],
    )


def solution(mesh):
    return jax.shard_map(
        local,
        mesh=mesh,
        in_specs=(
            P("dp", "seq", None),
            P("dp", "seq"),
            P("dp", "seq"),
            P("dp", "seq"),
            P("dp", "seq"),
            P("dp", "seq"),
            P("dp", "seq"),
            P("dp", "seq"),
            P("dp", "seq"),
            P(("dp", "seq")),
            P("dp", "seq", None),
        ),
        out_specs=(
            P("dp", "seq", None),
            P("dp", "seq", None),
            P("dp", "seq"),
            P("dp", "seq"),
            P("dp", "seq"),
            P("dp", "seq"),
            P("dp", "seq"),
            P("dp", "seq"),
            P("dp", "seq"),
            P(("dp", "seq")),
        ),
        check_vma=False,
    )
```

```python
from functools import partial
import math

import jax
import jax.numpy as jnp
from jax import lax
from jax.sharding import PartitionSpec as P

D = 640
NQ = 4
HD = 256
FF = 2048
WINDOW = 512
MICRO = 1


EPSILON = 1e-06
MASKED = -1e30


def shifted(block, axis, distance):
    devices = range(lax.axis_size(axis))
    route = [(i - distance, i) for i in devices if i - distance in devices]
    return lax.ppermute(block, axis, route)


def steps_of(axis):
    return lax.axis_size(axis).bit_length() - 1


def swapped(block, axis, step):
    route = [(i, i ^ (1 << step)) for i in range(lax.axis_size(axis))]
    return lax.ppermute(block, axis, route), (lax.axis_index(axis) >> step) & 1


def rms_scale(values, scales):
    mean_square = jnp.mean(values * values, axis=-1, keepdims=True)
    return values * lax.rsqrt(mean_square + EPSILON) * scales


def rotate(values, cosine, sine_table):
    middle = values.shape[-1] // 2
    turned = jnp.concatenate([-values[..., middle:], values[..., :middle]], axis=-1)
    return values * cosine + turned * sine_table


def query_map(raw_part, scales, cosine, sine_table):
    return rotate(rms_scale(raw_part, scales), cosine, sine_table) * (
        1.0 / math.sqrt(raw_part.shape[-1])
    )


def key_map(raw_part, scales, cosine, sine_table):
    return rotate(rms_scale(raw_part, scales), cosine, sine_table)


def gated_inner(gate_part, up_part):
    return jax.nn.gelu(gate_part, approximate=True) * up_part


def rotary_tables(positions, head_width):
    frequency = jnp.exp(
        jnp.arange(head_width // 2, dtype=jnp.float32) * (-2.0 * math.log(10000.0) / head_width)
    )
    angles = positions.astype(jnp.float32)[:, None] * frequency[None, :]
    angles = jnp.concatenate([angles, angles], axis=-1)
    return (jnp.cos(angles), jnp.sin(angles))


def rows_product(left_side, right_side):
    return lax.dot_general(
        left_side, right_side, (((0,), (0,)), ((), ())), preferred_element_type=jnp.float32
    )


def times_transposed(left_side, right_side):
    return lax.dot_general(
        left_side, right_side, (((1,), (1,)), ((), ())), preferred_element_type=jnp.float32
    )


def plain_product(left_side, right_side):
    return jnp.dot(left_side, right_side, preferred_element_type=jnp.float32)


def local(
    tokens_in,
    segment_ids,
    query_weight,
    key_weight,
    value_weight,
    out_weight,
    gate_weight,
    up_weight,
    down_weight,
    norm_gains,
    d_output,
):
    seqs_here = tokens_in.shape[0]
    block_len = tokens_in.shape[1]
    per_batch = seqs_here // MICRO
    token_count = per_batch * block_len
    seq_place = lax.axis_index("seq")
    positions = seq_place * block_len + jnp.arange(block_len, dtype=jnp.int32)
    cosine, sine_table = rotary_tables(positions, HD)
    prior_ids = shifted(segment_ids, "seq", 1)
    key_ids = jnp.concatenate([prior_ids, segment_ids], axis=1)
    row_index = jnp.arange(block_len, dtype=jnp.int32)[:, None]
    col_index = jnp.arange(2 * block_len, dtype=jnp.int32)[None, :]
    distance = row_index + block_len - col_index
    reach = (distance >= 0) & (distance < WINDOW) & ((col_index >= block_len) | (seq_place > 0))
    allowed_all = reach[None] & (segment_ids[:, :, None] == key_ids[:, None, :])

    dp_size = lax.axis_size("dp")
    seq_size = lax.axis_size("seq")

    def doubled(block, axis):
        for step in reversed(range(steps_of(axis))):
            other, mine = swapped(block, axis, step)
            block = jnp.where(
                mine == 0,
                jnp.concatenate([block, other], axis=0),
                jnp.concatenate([other, block], axis=0),
            )
        return block

    def ordered(block):
        shape = block.shape[1:]
        bits = steps_of("dp") + steps_of("seq")
        block = block.reshape((2,) * bits + shape)
        seq_dims = tuple(reversed(range(steps_of("seq"))))
        dp_dims = tuple(reversed(range(steps_of("seq"), bits)))
        block = block.transpose(seq_dims + dp_dims + (bits, bits + 1))
        return block.reshape((seq_size, dp_size) + shape)

    def gathered(block):
        return ordered(doubled(doubled(block[None], "dp"), "seq"))

    def columns_joined(stack):
        return stack.transpose(1, 2, 0, 3).reshape(dp_size * stack.shape[2], -1)

    def rows_joined(stack):
        return stack.transpose(0, 2, 1, 3).reshape(seq_size * stack.shape[2], -1)

    def fetch_weights():
        rows_in = query_weight.shape[0]
        query_cols = query_weight.shape[1]
        key_cols = key_weight.shape[1]
        width = query_cols + 2 * key_cols
        gain_rows = -(-norm_gains.shape[0] // width)
        gain_rows = -(-gain_rows // 16) * 16
        gain_block = jnp.pad(norm_gains, (0, gain_rows * width - norm_gains.shape[0])).reshape(
            gain_rows, width
        )
        first = jnp.concatenate(
            [jnp.concatenate([query_weight, key_weight, value_weight], axis=1), gain_block], axis=0
        )
        first = doubled(first[None], "dp")
        second = out_weight.T
        third = jnp.concatenate([gate_weight, up_weight], axis=1)
        fourth = down_weight.T
        first, second, third, fourth = lax.optimization_barrier((first, second, third, fourth))
        first = ordered(doubled(first, "seq"))
        second = gathered(second)
        third = gathered(third)
        fourth = gathered(fourth)
        half = gate_weight.shape[1]
        gains_all = first[:, :, rows_in:].reshape(seq_size, dp_size, -1)[..., : norm_gains.shape[0]]
        return (
            columns_joined(first[:, :, :rows_in, :query_cols]),
            columns_joined(first[:, :, :rows_in, query_cols : query_cols + key_cols]),
            columns_joined(first[:, :, :rows_in, query_cols + key_cols :]),
            rows_joined(second),
            columns_joined(third[..., :half]),
            columns_joined(third[..., half:]),
            rows_joined(fourth),
            gains_all.transpose(1, 0, 2).reshape(-1),
        )

    weights_all = fetch_weights()

    def halve(block, axis, step):
        block = block.reshape((-1, 2) + block.shape[1:])
        mine = (lax.axis_index(axis) >> step) & 1
        away = jnp.where(mine == 0, block[:, 1], block[:, 0])
        kept = jnp.where(mine == 0, block[:, 0], block[:, 1])
        other, _ = swapped(away, axis, step)
        return (kept.astype(jnp.float32) + other.astype(jnp.float32)).astype(jnp.bfloat16)

    def halved(block, axis, first_step=0):
        for step in range(first_step, steps_of(axis)):
            block = halve(block, axis, step)
        return block[0]

    def tied(value, *blocks):
        return lax.optimization_barrier((value,) + blocks)

    def seq_summed(block):
        return halved(block, "seq")

    def dp_summed(block):
        return halved(block, "dp")

    def seq_split(block):
        return block.astype(jnp.bfloat16).reshape(seq_size, -1, block.shape[1])

    def dp_split(block):
        return block.reshape(block.shape[0], dp_size, -1).transpose(1, 0, 2)

    out_blocks = []
    grad_blocks = []
    for micro_index in range(MICRO):
        row_lower = micro_index * per_batch
        row_upper = row_lower + per_batch
        weights_now = weights_all
        gains_float = weights_now[7].astype(jnp.float32)
        in_scale = gains_float[0:D]
        attn_scale = gains_float[D : 2 * D]
        pre_scale = gains_float[2 * D : 3 * D]
        post_scale = gains_float[3 * D : 4 * D]
        query_scale = gains_float[4 * D : 4 * D + HD]
        key_scale = gains_float[4 * D + HD : 4 * D + 2 * HD]
        tokens_now = tokens_in[row_lower:row_upper].astype(jnp.float32).reshape(token_count, D)
        normed_vals, input_pull = jax.vjp(rms_scale, tokens_now, in_scale)
        normed = normed_vals.astype(jnp.bfloat16)
        query_raw = plain_product(normed, weights_now[0]).reshape(per_batch, block_len, NQ, HD)
        key_raw = plain_product(normed, weights_now[1]).reshape(per_batch, block_len, HD)
        values_own = (
            plain_product(normed, weights_now[2])
            .astype(jnp.bfloat16)
            .reshape(per_batch, block_len, HD)
        )
        query_vals, query_pull = jax.vjp(
            partial(query_map, cosine=cosine[:, None, :], sine_table=sine_table[:, None, :]),
            query_raw,
            query_scale,
        )
        key_vals, key_pull = jax.vjp(
            partial(key_map, cosine=cosine, sine_table=sine_table), key_raw, key_scale
        )
        queries = query_vals.astype(jnp.bfloat16)
        keys_own = key_vals.astype(jnp.bfloat16)
        prior_pair = shifted(jnp.concatenate([keys_own, values_own], axis=-1), "seq", 1)
        keys_all = jnp.concatenate([prior_pair[..., :HD], keys_own], axis=1)
        values_all = jnp.concatenate([prior_pair[..., HD:], values_own], axis=1)
        allowed = allowed_all[row_lower:row_upper][:, None]
        scores = jnp.einsum("sqhd,skd->shqk", queries, keys_all, preferred_element_type=jnp.float32)
        scores = jnp.where(allowed, scores, MASKED)
        row_top = jnp.max(scores, axis=-1, keepdims=True)
        weights_exp = jnp.exp(scores - row_top)
        row_total = jnp.sum(weights_exp, axis=-1, keepdims=True)
        prob_weights = (weights_exp / row_total).astype(jnp.bfloat16)
        mixed_heads = jnp.einsum(
            "shqk,skd->sqhd", prob_weights, values_all, preferred_element_type=jnp.float32
        )
        mixed_heads = mixed_heads.astype(jnp.bfloat16).reshape(token_count, NQ * HD)
        branch = times_transposed(mixed_heads, weights_now[3])
        post_vals, post_pull = jax.vjp(rms_scale, branch, attn_scale)
        residual = tokens_now + post_vals
        inner_vals, inner_pull = jax.vjp(rms_scale, residual, pre_scale)
        inner_normed = inner_vals.astype(jnp.bfloat16)
        gate_vals = plain_product(inner_normed, weights_now[4])
        up_vals = plain_product(inner_normed, weights_now[5])
        hidden_vals, hidden_pull = jax.vjp(gated_inner, gate_vals, up_vals)
        hidden = hidden_vals.astype(jnp.bfloat16)
        ffn_vals = times_transposed(hidden, weights_now[6])
        final_vals, final_pull = jax.vjp(rms_scale, ffn_vals, post_scale)
        out_blocks.append(
            (residual + final_vals).astype(jnp.bfloat16).reshape(per_batch, block_len, D)
        )
        weights_back = weights_all
        cotangent = d_output[row_lower:row_upper].astype(jnp.float32).reshape(token_count, D)
        d_ffn, d_post_scale = final_pull(cotangent)
        d_ffn = d_ffn.astype(jnp.bfloat16)
        grad_down = halve(seq_split(rows_product(d_ffn, hidden)), "seq", 0)
        d_hidden = plain_product(d_ffn, weights_back[6])
        d_gate, d_up = hidden_pull(d_hidden)
        d_gate = d_gate.astype(jnp.bfloat16)
        d_up = d_up.astype(jnp.bfloat16)
        grad_pair = halve(
            jnp.concatenate(
                [
                    seq_split(rows_product(d_gate, inner_normed)),
                    seq_split(rows_product(d_up, inner_normed)),
                ],
                axis=1,
            ),
            "seq",
            0,
        )
        d_inner = times_transposed(d_gate, weights_back[4]) + times_transposed(
            d_up, weights_back[5]
        )
        d_resid_part, d_pre_scale = inner_pull(d_inner)
        d_resid = cotangent + d_resid_part
        d_branch, d_attn_scale = post_pull(d_resid)
        d_branch = d_branch.astype(jnp.bfloat16)
        d_branch, grad_down, grad_pair = tied(d_branch, grad_down, grad_pair)
        grad_down = halved(grad_down, "seq", 1)
        grad_pair = halved(grad_pair, "seq", 1)
        grad_out = halve(seq_split(rows_product(d_branch, mixed_heads)), "seq", 0)
        d_mixed = (
            plain_product(d_branch, weights_back[3])
            .astype(jnp.bfloat16)
            .reshape(per_batch, block_len, NQ, HD)
        )
        scores_again = jnp.einsum(
            "sqhd,skd->shqk", queries, keys_all, preferred_element_type=jnp.float32
        )
        scores_again = jnp.where(allowed, scores_again, MASKED)
        probs_float = jnp.exp(scores_again - row_top) / row_total
        probs_again = probs_float.astype(jnp.bfloat16)
        d_probs = jnp.einsum(
            "sqhd,skd->shqk", d_mixed, values_all, preferred_element_type=jnp.float32
        )
        row_inner = jnp.sum(probs_float * d_probs, axis=-1, keepdims=True)
        d_scores = (probs_float * (d_probs - row_inner)).astype(jnp.bfloat16)
        d_scores, grad_down, grad_pair, grad_out = tied(d_scores, grad_down, grad_pair, grad_out)
        grad_out = halved(grad_out, "seq", 1)
        grad_down = halve(dp_split(grad_down), "dp", 0)
        grad_pair = halve(grad_pair.T.reshape(dp_size, D // dp_size, -1), "dp", 0)
        d_queries = jnp.einsum(
            "shqk,skd->sqhd", d_scores, keys_all, preferred_element_type=jnp.float32
        )
        d_keys = jnp.einsum("shqk,sqhd->skd", d_scores, queries, preferred_element_type=jnp.float32)
        d_values = jnp.einsum(
            "shqk,sqhd->skd", probs_again, d_mixed, preferred_element_type=jnp.float32
        )
        earlier_part = jnp.concatenate([d_keys[:, :block_len], d_values[:, :block_len]], axis=-1).astype(jnp.bfloat16)
        later_pair = shifted(earlier_part, "seq", -1)
        d_keys_own = d_keys[:, block_len:] + later_pair[..., :HD]
        d_values_own = (
            (d_values[:, block_len:] + later_pair[..., HD:])
            .astype(jnp.bfloat16)
            .reshape(token_count, HD)
        )
        d_query_raw, d_query_scale = query_pull(d_queries)
        d_query_raw = d_query_raw.astype(jnp.bfloat16).reshape(token_count, NQ * HD)
        d_query_raw, grad_down, grad_pair, grad_out = tied(
            d_query_raw, grad_down, grad_pair, grad_out
        )
        grad_out = halve(dp_split(grad_out), "dp", 0)
        grad_down = halved(grad_down, "dp", 1)
        grad_pair = halved(grad_pair, "dp", 1)
        d_key_raw, d_key_scale = key_pull(d_keys_own)
        d_key_raw = d_key_raw.astype(jnp.bfloat16).reshape(token_count, HD)
        grad_query = rows_product(d_query_raw, normed)
        grad_key = rows_product(d_key_raw, normed)
        grad_value = rows_product(d_values_own, normed)
        d_normed = (
            times_transposed(d_query_raw, weights_back[0])
            + times_transposed(d_key_raw, weights_back[1])
            + times_transposed(d_values_own, weights_back[2])
        )
        d_tokens, d_in_scale = input_pull(d_normed)
        grad_blocks.append((d_resid + d_tokens).reshape(per_batch, block_len, D))
        grad_gains = jnp.concatenate(
            [d_in_scale, d_attn_scale, d_pre_scale, d_post_scale, d_query_scale, d_key_scale]
        )
    output = jnp.concatenate(out_blocks, axis=0)
    grad_input = jnp.concatenate(grad_blocks, axis=0)
    gain_count = norm_gains.shape[0]
    gain_rows = -(-(dp_size * gain_count) // (16 * D)) * 16
    gain_part = grad_gains.reshape(dp_size, seq_size, gain_count).transpose(1, 0, 2)
    gain_part = jnp.pad(
        gain_part.reshape(seq_size, -1), ((0, 0), (0, gain_rows * D - dp_size * gain_count))
    ).reshape(seq_size, gain_rows, D)
    last = seq_summed(
        jnp.concatenate(
            [
                seq_split(grad_query),
                seq_split(grad_key),
                seq_split(grad_value),
                gain_part.astype(jnp.bfloat16),
            ],
            axis=1,
        )
    )
    width = last.shape[0] - gain_rows
    gain_now = last[width:].reshape(-1)[: dp_size * gain_count].reshape(dp_size, gain_count)
    extra = -(-gain_count // (16 * width)) * 16
    gain_now = jnp.pad(gain_now, ((0, 0), (0, extra * width - gain_count)))
    last = jnp.concatenate(
        [
            last[:width].T.reshape(dp_size, D // dp_size, width),
            gain_now.reshape(dp_size, extra, width),
        ],
        axis=1,
    )
    last = dp_summed(last).astype(jnp.float32)
    rows_in = query_weight.shape[0]
    query_cols = query_weight.shape[1]
    key_cols = key_weight.shape[1]
    half = gate_weight.shape[1]
    pair_done = grad_pair.astype(jnp.float32)
    out_done = halved(grad_out, "dp", 1).astype(jnp.float32).T
    down_done = grad_down.astype(jnp.float32).T
    return (
        output,
        grad_input,
        last[:rows_in, :query_cols],
        last[:rows_in, query_cols : query_cols + key_cols],
        last[:rows_in, query_cols + key_cols :],
        out_done,
        pair_done[:, :half],
        pair_done[:, half:],
        down_done,
        last[rows_in:].reshape(-1)[:gain_count],
    )


def solution(mesh):
    return jax.shard_map(
        local,
        mesh=mesh,
        in_specs=(
            P("dp", "seq", None),
            P("dp", "seq"),
            P("dp", "seq"),
            P("dp", "seq"),
            P("dp", "seq"),
            P("dp", "seq"),
            P("dp", "seq"),
            P("dp", "seq"),
            P("dp", "seq"),
            P(("dp", "seq")),
            P("dp", "seq", None),
        ),
        out_specs=(
            P("dp", "seq", None),
            P("dp", "seq", None),
            P("dp", "seq"),
            P("dp", "seq"),
            P("dp", "seq"),
            P("dp", "seq"),
            P("dp", "seq"),
            P("dp", "seq"),
            P("dp", "seq"),
            P(("dp", "seq")),
        ),
        check_vma=False,
    )
```
